32 devices in a mesh: groups: 2 (over x), tm: 16 (over z, y, core).
Axes of the slice: x: 2, y: 2, z: 4, core: 2. Of those that a mesh axis runs over, the one named last changes fastest.
Arguments:
- intensity: bfloat16 [64, 24576], P(('groups', 'tm')), parts along dimension 0, may hold values from 0.19921875 to 5
- cycle_label: int32 [49152], P('groups'), parts along dimension 0, may hold values from 0 to 71, as said below
- pixel_mask: int32 [49152], P('groups'), parts along dimension 0, may hold values from 0 to 1, as said below
- pair_table: int32 [16, 16], replicated, may hold values from 0 to 1, as said below
Outputs:
- two_time: float32 [64, 72, 32], P(('groups', 'tm')), parts along dimension 0
The draws below stay inside these ranges and needn't reach their ends.
There are 2 independent parts, one for each index of `groups`. The reference program is written for one: setup_inputs(seed, part) draws one part's arguments, and reference() takes and returns one part's arrays. A program takes and returns all parts, laid end to end along the dimension named above; an argument that names none is the same for every part. Nothing has to cross between parts.
Inputs may be any that keep to these rules, and one draw needn't show every extreme that they name: `cycle_label`: pixel labels lie in 0 to 71; every cycle holds at least one live pixel. `pixel_mask`: every cycle holds at least one pixel whose mask is 1. `pair_table`: Symmetric, with ones on the diagonal.
All inputs are finite; a program needn't handle non-finite values.
Results may differ from the reference program's by a relative error of at most 0.0003.
Values may be sent and summed in bfloat16 or wider, within the bound.
A program may use at most 128 MiB of HBM per device.

```python
import math
import jax
import jax.numpy as jnp
from jax import lax

CYCLES = 72
FRAMES = 32
PIXELS = 24576
FRAME_BLOCKS = 16


def draw_cycle_label(key, part):
    key = jax.random.fold_in(key, 11)
    position = jnp.arange(PIXELS, dtype=jnp.int32)
    spread = max(CYCLES // 6, 1)
    noise = jax.random.randint(key, (PIXELS,), -spread, spread + 1)
    label = jnp.clip(position * CYCLES // PIXELS + noise, 0, CYCLES - 1).astype(jnp.int32)
    stride = PIXELS // CYCLES
    anchor = jnp.arange(CYCLES, dtype=jnp.int32) * stride + stride // 2
    return label.at[anchor].set(jnp.arange(CYCLES, dtype=jnp.int32))


def draw_pixel_mask(key, part):
    key = jax.random.fold_in(key, 12)
    position = jnp.arange(PIXELS, dtype=jnp.int32)
    ticket = jax.random.randint(key, (PIXELS,), 0, 10 * PIXELS)
    alive = (ticket < 3 * PIXELS + 6 * position).astype(jnp.int32)
    stride = PIXELS // CYCLES
    anchor = jnp.arange(CYCLES, dtype=jnp.int32) * stride + stride // 2
    return alive.at[anchor].set(1)


def draw_pair_table(key, part):
    key = jax.random.fold_in(key, 13)
    draws = jax.random.randint(key, (FRAME_BLOCKS, FRAME_BLOCKS), 0, 3)
    row_ids = jnp.arange(FRAME_BLOCKS, dtype=jnp.int32)[:, None]
    col_ids = jnp.arange(FRAME_BLOCKS, dtype=jnp.int32)[None, :]
    mirrored = jnp.where(row_ids <= col_ids, draws, jnp.transpose(draws))
    near = jnp.abs(row_ids - col_ids) <= FRAME_BLOCKS // 8
    return jnp.where(near | (mirrored == 0), 1, 0).astype(jnp.int32)


def levels(key, dims, pieces, low, top_value):
    gain, own = 1.0, jax.random.fold_in(key, 6)
    for dim, blocks in pieces:
        steps = jnp.exp(jax.random.uniform(jax.random.fold_in(own, dim), (blocks,), jnp.float32, low / len(pieces), top_value / len(pieces)))
        gain = gain * jnp.repeat(steps, dims[dim] // blocks).reshape([-1 if axis == dim else 1 for axis in range(len(dims))])
    return gain


def setup_inputs(seed: int = 0, part: int = 0) -> dict:
    splits = jax.random.split(jax.random.key(seed), 5)
    part_splits = jax.random.split(jax.random.fold_in(splits[4], part), 5)
    intensity = jnp.clip(jnp.exp(math.log(5.0) - 3.2227897 * jax.random.uniform(part_splits[0], (FRAMES, PIXELS), jnp.float32) ** levels(part_splits[0], (FRAMES, PIXELS), ((0, 16),), -0.2, 0.2)), 0.19921875, 5.0).astype(jnp.bfloat16)
    cycle_label = draw_cycle_label(jax.random.fold_in(jax.random.fold_in(splits[4], part), 71), part)
    pixel_mask = draw_pixel_mask(jax.random.fold_in(jax.random.fold_in(splits[4], part), 71), part)
    pair_table = draw_pair_table(jax.random.fold_in(splits[4], 71), part)
    return dict(intensity=intensity, cycle_label=cycle_label, pixel_mask=pixel_mask, pair_table=pair_table)


def reference(intensity, cycle_label, pixel_mask, pair_table):
    values = intensity.astype(jnp.float32)
    live_pixel = pixel_mask.astype(jnp.float32)
    weighted = values * live_pixel[None, :]

    def one_frame(frame_row):
        return jax.ops.segment_sum(jnp.transpose(weighted * frame_row[None, :]), cycle_label, num_segments=CYCLES)

    cycle_grams = lax.map(one_frame, values)
    cycle_sums = jax.ops.segment_sum(jnp.transpose(weighted), cycle_label, num_segments=CYCLES)
    counts = jax.ops.segment_sum(live_pixel, cycle_label, num_segments=CYCLES)
    frames_per = values.shape[0] // pair_table.shape[0]
    pair_keep = jnp.repeat(jnp.repeat(pair_table.astype(jnp.float32), frames_per, axis=0), frames_per, axis=1)
    denominator = jnp.transpose(cycle_sums)[:, :, None] * cycle_sums[None, :, :]
    return cycle_grams * counts[None, :, None] / denominator * pair_keep[:, None, :]
```

```python
import functools

import jax
import jax.numpy as jnp
from jax import lax
from jax.experimental import pallas as pl
from jax.experimental.pallas import tpu as pltpu
from jax.sharding import PartitionSpec as P

CYCLES = 72
GROUPS8 = CYCLES // 8
LANES = 128
NT = (((1,), (1,)), ((), ()))


def member_of(label, mask):
    key = jnp.where(mask == 1, label, -1)
    ids = lax.broadcasted_iota(jnp.int32, (CYCLES, label.shape[1]), 0)
    return jnp.where(key == ids, 1.0, 0.0).astype(jnp.bfloat16)


def kernel(
    n, x_ref, label_ref, mask_ref, pair_ref, out_ref,
    pixels, frames32, part_out, part_in, stat_out, stat_in, stat_all, ones8, member_own,
    send1, recv1, send2, recv2, send3, recv3,
):
    me = lax.axis_index("tm")
    per, total = x_ref.shape
    share = total // n
    frames = n * per
    pack = max(LANES // frames, 1)

    def peer(step):
        sign = 1 - 2 * lax.rem(step, 2)
        return lax.rem(me + n // 2 + sign * ((step + 1) // 2) + n, n)

    def share_of(device):
        return pl.ds(pl.multiple_of(device * share, LANES), share)

    def pixel_copy(device, slot):
        return pltpu.make_async_remote_copy(
            src_ref=x_ref.at[:, share_of(device)],
            dst_ref=pixels.at[slot],
            send_sem=send1.at[device],
            recv_sem=recv1.at[slot],
            device_id={"tm": device},
            device_id_type=pl.DeviceIdType.MESH,
        )

    def stat_copy(device, slot):
        return pltpu.make_async_remote_copy(
            src_ref=stat_out,
            dst_ref=stat_in.at[slot],
            send_sem=send3.at[device],
            recv_sem=recv3.at[slot],
            device_id={"tm": device},
            device_id_type=pl.DeviceIdType.MESH,
        )

    def part_copy(device, slot):
        return pltpu.make_async_remote_copy(
            src_ref=part_out.at[device],
            dst_ref=part_in.at[slot],
            send_sem=send2.at[device],
            recv_sem=recv2.at[slot],
            device_id={"tm": device},
            device_id_type=pl.DeviceIdType.MESH,
        )

    barrier = pltpu.get_barrier_semaphore()

    def greet(step, _):
        pl.semaphore_signal(
            barrier, inc=1, device_id={"tm": peer(step)}, device_id_type=pl.DeviceIdType.MESH
        )
        return 0

    lax.fori_loop(0, n - 1, greet, 0)
    pl.semaphore_wait(barrier, n - 1)

    def send_pixels(step, _):
        pixel_copy(peer(step), me).start()
        return 0

    lax.fori_loop(0, n - 1, send_pixels, 0)

    pixels[me] = x_ref[:, share_of(me)]
    ones8[...] = jnp.ones_like(ones8)

    def local_sums(block, running):
        where = share_of(block)
        member = member_of(label_ref[:, where], mask_ref[:, where])
        ones8[:per] = x_ref[:, where].astype(jnp.float32)
        return running + lax.dot_general(
            ones8[...].astype(jnp.bfloat16), member, NT, preferred_element_type=jnp.float32
        )

    stats = lax.fori_loop(0, n, local_sums, jnp.zeros((8, CYCLES), jnp.float32))
    stat_out[...] = jnp.zeros_like(stat_out)
    stat_out[:, :CYCLES] = stats
    stat_in[me] = stat_out[...]

    def send_stats(step, _):
        stat_copy(peer(step), me).start()
        return 0

    lax.fori_loop(0, n - 1, send_stats, 0)

    member_own[...] = member_of(label_ref[:, share_of(me)], mask_ref[:, share_of(me)])

    def take_pixels(step, _):
        pixel_copy(peer(step), peer(step)).wait_recv()
        return 0

    lax.fori_loop(0, n - 1, take_pixels, 0)
    for device in range(n):
        frames32[device * per : (device + 1) * per] = pixels[device].astype(jnp.float32)
    right = frames32[...].astype(jnp.bfloat16)

    def partial(device):
        rows = pixels[device].astype(jnp.float32)
        grams = []
        for f in range(per):
            weighted = member_own[...] * rows[f : f + 1].astype(jnp.bfloat16)
            grams.append(lax.dot_general(weighted, right, NT, preferred_element_type=jnp.float32))
        tiles = [g[8 * c : 8 * c + 8] for g in grams for c in range(GROUPS8)]
        while len(tiles) % pack:
            tiles.append(jnp.zeros((8, frames), jnp.float32))
        return [jnp.concatenate(tiles[i : i + pack], axis=1) for i in range(0, len(tiles), pack)]

    def send_part(step, _):
        device = peer(step)
        for i, tile in enumerate(partial(device)):
            part_out[device, 8 * i : 8 * i + 8] = tile
        part_copy(device, me).start()
        return 0

    lax.fori_loop(0, n - 1, send_part, 0)
    for i, tile in enumerate(partial(me)):
        part_in[me, 8 * i : 8 * i + 8] = tile

    def take_stats(step, _):
        stat_copy(peer(step), peer(step)).wait_recv()
        return 0

    lax.fori_loop(0, n - 1, take_stats, 0)
    for device in range(n):
        stat_all[device * per : (device + 1) * per] = stat_in[device, :per]
    sums = jnp.transpose(stat_all[...])[:CYCLES]
    own = jnp.transpose(stat_out[...])[:CYCLES]
    blocks = lax.broadcasted_iota(jnp.int32, (n, frames), 0)
    owners = lax.broadcasted_iota(jnp.int32, (n, frames), 1) // per
    spread = jnp.where(blocks == owners, 1.0, 0.0)
    table = pair_ref[...].astype(jnp.float32)
    mine = jnp.where(lax.broadcasted_iota(jnp.int32, (n, n), 0) == me, table, 0.0)
    keep_row = jnp.sum(mine, axis=0, keepdims=True)
    keep = lax.dot_general(
        jnp.broadcast_to(keep_row, (8, n)).astype(jnp.bfloat16),
        spread.astype(jnp.bfloat16),
        (((1,), (0,)), ((), ())),
        preferred_element_type=jnp.float32,
    )[:1]
    counts = own[:, per : per + 1]
    factors = [counts * keep / (own[:, f : f + 1] * sums) for f in range(per)]

    def take_parts(step, _):
        part_copy(peer(step), peer(step)).wait_recv()
        return 0

    lax.fori_loop(0, n - 1, take_parts, 0)
    for i in range(part_in.shape[1] // 8):
        tile = part_in[0, 8 * i : 8 * i + 8]
        for device in range(1, n):
            tile = tile + part_in[device, 8 * i : 8 * i + 8]
        for b in range(pack):
            f, c = divmod(i * pack + b, GROUPS8)
            if f < per:
                gram = tile[:, b * frames : (b + 1) * frames]
                out_ref[f, 8 * c : 8 * c + 8] = gram * factors[f][8 * c : 8 * c + 8]

    def settle(step, _):
        pixel_copy(peer(step), me).wait_send()
        stat_copy(peer(step), me).wait_send()
        part_copy(peer(step), me).wait_send()
        return 0

    lax.fori_loop(0, n - 1, settle, 0)


def on_device(n, intensity, cycle_label, pixel_mask, pair_table):
    per, total = intensity.shape
    share = total // n
    frames = n * per
    pack = max(LANES // frames, 1)
    rows = -(-per * GROUPS8 // pack) * 8
    width = pack * frames
    vmem = pl.BlockSpec(memory_space=pltpu.VMEM)
    sems = pltpu.SemaphoreType.DMA((n,))
    return pl.pallas_call(
        functools.partial(kernel, n),
        out_shape=jax.ShapeDtypeStruct((per, CYCLES, frames), jnp.float32),
        in_specs=[vmem] * 4,
        out_specs=vmem,
        scratch_shapes=[
            pltpu.VMEM((n, per, share), jnp.bfloat16),
            pltpu.VMEM((frames, share), jnp.float32),
            pltpu.VMEM((n, rows, width), jnp.float32),
            pltpu.VMEM((n, rows, width), jnp.float32),
            pltpu.VMEM((8, LANES), jnp.float32),
            pltpu.VMEM((n, 8, LANES), jnp.float32),
            pltpu.VMEM((frames, LANES), jnp.float32),
            pltpu.VMEM((8, share), jnp.float32),
            pltpu.VMEM((CYCLES, share), jnp.bfloat16),
            sems, sems, sems, sems, sems, sems,
        ],
        compiler_params=pltpu.CompilerParams(
            collective_id=0, has_side_effects=True, vmem_limit_bytes=40 * 1024 * 1024
        ),
    )(intensity, cycle_label.reshape(1, total), pixel_mask.reshape(1, total), pair_table)


def solution(mesh):
    in_specs = (P(("groups", "tm"), None), P("groups"), P("groups"), P())
    out_specs = P(("groups", "tm"), None, None)
    return jax.shard_map(
        functools.partial(on_device, mesh.shape["tm"]),
        mesh=mesh, in_specs=in_specs, out_specs=out_specs, check_vma=False,
    )
```

```python
import functools

import jax
import jax.numpy as jnp
from jax import lax
from jax.experimental import pallas as pl
from jax.experimental.pallas import tpu as pltpu
from jax.sharding import PartitionSpec as P

CYCLES = 72
GROUPS8 = CYCLES // 8
LANES = 128
NT = (((1,), (1,)), ((), ()))


def member_of(label, mask):
    key = jnp.where(mask == 1, label, -1)
    ids = lax.broadcasted_iota(jnp.int32, (CYCLES, label.shape[1]), 0)
    return jnp.where(key == ids, 1.0, 0.0).astype(jnp.bfloat16)


def kernel(
    n, x_hbm, label_hbm, mask_hbm, pair_hbm, out_ref,
    x_ref, label_ref, mask_ref, pair_ref, pixels, frames32, part_out, part_in, stat_out, stat_in, stat_all, ones8, member_own,
    load, send1, recv1, send2, recv2, send3, recv3,
):
    me = lax.axis_index("tm")
    per, total = x_hbm.shape
    share = total // n
    frames = n * per
    pack = max(LANES // frames, 1)

    def peer(step):
        there = me + step
        return jnp.where(there >= n, there - n, there)

    def all_of(buffer, sem):
        blocks = buffer.at[pl.ds(0, n - 1)]
        pltpu.make_async_copy(blocks, blocks, sem).wait()

    def share_of(device):
        return pl.ds(pl.multiple_of(device * share, LANES), share)

    def pixel_copy(device, slot):
        return pltpu.make_async_remote_copy(
            src_ref=x_hbm.at[:, share_of(device)],
            dst_ref=pixels.at[slot],
            send_sem=send1,
            recv_sem=recv1,
            device_id={"tm": device},
            device_id_type=pl.DeviceIdType.MESH,
        )

    def stat_copy(device, slot):
        return pltpu.make_async_remote_copy(
            src_ref=stat_out,
            dst_ref=stat_in.at[slot],
            send_sem=send3,
            recv_sem=recv3,
            device_id={"tm": device},
            device_id_type=pl.DeviceIdType.MESH,
        )

    def part_copy(device, slot):
        return pltpu.make_async_remote_copy(
            src_ref=part_out.at[device],
            dst_ref=part_in.at[slot],
            send_sem=send2,
            recv_sem=recv2,
            device_id={"tm": device},
            device_id_type=pl.DeviceIdType.MESH,
        )

    loads = [
        pltpu.make_async_copy(source, target, load.at[i])
        for i, (source, target) in enumerate(
            [(label_hbm, label_ref), (mask_hbm, mask_ref), (x_hbm, x_ref), (pair_hbm, pair_ref)]
        )
    ]
    for copy in loads:
        copy.start()
    barrier = pltpu.get_barrier_semaphore()

    for step in range(1, n):
        pl.semaphore_signal(
            barrier, inc=1, device_id={"tm": peer(step)}, device_id_type=pl.DeviceIdType.MESH
        )
    pl.semaphore_wait(barrier, n - 1)
    for step in range(1, n):
        pixel_copy(peer(step), me).start()
    for copy in loads:
        copy.wait()

    pixels[me] = x_ref[:, share_of(me)]
    ones8[...] = jnp.ones_like(ones8)

    def local_sums(block, running):
        where = share_of(block)
        member = member_of(label_ref[:, where], mask_ref[:, where])
        ones8[:per] = x_ref[:, where].astype(jnp.float32)
        return running + lax.dot_general(
            ones8[...].astype(jnp.bfloat16), member, NT, preferred_element_type=jnp.float32
        )

    stats = lax.fori_loop(0, n, local_sums, jnp.zeros((8, CYCLES), jnp.float32))
    stat_out[...] = jnp.zeros_like(stat_out)
    stat_out[:, :CYCLES] = stats
    stat_in[me] = stat_out[...]
    member_own[...] = member_of(label_ref[:, share_of(me)], mask_ref[:, share_of(me)])


    for step in range(1, n):
        stat_copy(peer(step), me).start()

    all_of(pixels, recv1)
    for device in range(n):
        frames32[device * per : (device + 1) * per] = pixels[device].astype(jnp.float32)
    right = frames32[...].astype(jnp.bfloat16)

    def partial(device):
        rows = pixels[device].astype(jnp.float32)
        grams = []
        for f in range(per):
            weighted = member_own[...] * rows[f : f + 1].astype(jnp.bfloat16)
            grams.append(lax.dot_general(weighted, right, NT, preferred_element_type=jnp.float32))
        tiles = [g[8 * c : 8 * c + 8] for g in grams for c in range(GROUPS8)]
        while len(tiles) % pack:
            tiles.append(jnp.zeros((8, frames), jnp.float32))
        return [jnp.concatenate(tiles[i : i + pack], axis=1) for i in range(0, len(tiles), pack)]

    def send_part(step, _):
        device = peer(step)
        for i, tile in enumerate(partial(device)):
            part_out[device, 8 * i : 8 * i + 8] = tile
        part_copy(device, me).start()
        return 0

    lax.fori_loop(1, n, send_part, 0)
    for i, tile in enumerate(partial(me)):
        part_in[me, 8 * i : 8 * i + 8] = tile

    all_of(stat_in, recv3)
    for device in range(n):
        stat_all[device * per : (device + 1) * per] = stat_in[device, :per]
    sums = jnp.transpose(stat_all[...])[:CYCLES]
    own = jnp.transpose(stat_out[...])[:CYCLES]
    blocks = lax.broadcasted_iota(jnp.int32, (n, frames), 0)
    owners = lax.broadcasted_iota(jnp.int32, (n, frames), 1) // per
    spread = jnp.where(blocks == owners, 1.0, 0.0)
    table = pair_ref[...].astype(jnp.float32)
    mine = jnp.where(lax.broadcasted_iota(jnp.int32, (n, n), 0) == me, table, 0.0)
    keep_row = jnp.sum(mine, axis=0, keepdims=True)
    keep = lax.dot_general(
        jnp.broadcast_to(keep_row, (8, n)).astype(jnp.bfloat16),
        spread.astype(jnp.bfloat16),
        (((1,), (0,)), ((), ())),
        preferred_element_type=jnp.float32,
    )[:1]
    counts = own[:, per : per + 1]
    factors = [counts * keep / (own[:, f : f + 1] * sums) for f in range(per)]

    all_of(part_in, recv2)
    for i in range(part_in.shape[1] // 8):
        tile = part_in[0, 8 * i : 8 * i + 8]
        for device in range(1, n):
            tile = tile + part_in[device, 8 * i : 8 * i + 8]
        for b in range(pack):
            f, c = divmod(i * pack + b, GROUPS8)
            if f < per:
                gram = tile[:, b * frames : (b + 1) * frames]
                out_ref[f, 8 * c : 8 * c + 8] = gram * factors[f][8 * c : 8 * c + 8]

    all_of(pixels, send1)
    all_of(stat_in, send3)
    all_of(part_in, send2)


def on_device(n, intensity, cycle_label, pixel_mask, pair_table):
    per, total = intensity.shape
    share = total // n
    frames = n * per
    pack = max(LANES // frames, 1)
    rows = -(-per * GROUPS8 // pack) * 8
    width = pack * frames
    vmem = pl.BlockSpec(memory_space=pltpu.VMEM)
    sem = pltpu.SemaphoreType.DMA
    return pl.pallas_call(
        functools.partial(kernel, n),
        out_shape=jax.ShapeDtypeStruct((per, CYCLES, frames), jnp.float32),
        in_specs=[pl.BlockSpec(memory_space=pl.ANY)] * 4,
        out_specs=vmem,
        scratch_shapes=[
            pltpu.VMEM((per, total), jnp.bfloat16),
            pltpu.VMEM((1, total), jnp.int32),
            pltpu.VMEM((1, total), jnp.int32),
            pltpu.VMEM(pair_table.shape, jnp.int32),
            pltpu.VMEM((n, per, share), jnp.bfloat16),
            pltpu.VMEM((frames, share), jnp.float32),
            pltpu.VMEM((n, rows, width), jnp.float32),
            pltpu.VMEM((n, rows, width), jnp.float32),
            pltpu.VMEM((8, LANES), jnp.float32),
            pltpu.VMEM((n, 8, LANES), jnp.float32),
            pltpu.VMEM((frames, LANES), jnp.float32),
            pltpu.VMEM((8, share), jnp.float32),
            pltpu.VMEM((CYCLES, share), jnp.bfloat16),
            pltpu.SemaphoreType.DMA((4,)),
            sem, sem, sem, sem, sem, sem,
        ],
        compiler_params=pltpu.CompilerParams(
            collective_id=0, has_side_effects=True, vmem_limit_bytes=56 * 1024 * 1024
        ),
    )(intensity, cycle_label.reshape(1, total), pixel_mask.reshape(1, total), pair_table)


def solution(mesh):
    in_specs = (P(("groups", "tm"), None), P("groups"), P("groups"), P())
    out_specs = P(("groups", "tm"), None, None)
    return jax.shard_map(
        functools.partial(on_device, mesh.shape["tm"]),
        mesh=mesh, in_specs=in_specs, out_specs=out_specs, check_vma=False,
    )
```

```python
import functools

import jax
import jax.numpy as jnp
from jax import lax
from jax.experimental import pallas as pl
from jax.experimental.pallas import tpu as pltpu
from jax.sharding import PartitionSpec as P

CYCLES = 72
GROUPS8 = CYCLES // 8
LANES = 128
NT = (((1,), (1,)), ((), ()))


def member_of(label, mask):
    key = jnp.where(mask == 1, label, -1)
    ids = lax.broadcasted_iota(jnp.int32, (CYCLES, label.shape[1]), 0)
    return jnp.where(key == ids, 1.0, 0.0).astype(jnp.bfloat16)


def kernel(
    n, x_hbm, label_hbm, mask_hbm, pair_hbm, out_ref,
    x_ref, label_ref, mask_ref, pair_ref, pixels, frames32, part_out, part_in, stat_out, stat_in, stat_all, ones8, member_own,
    load, send1, recv1, send2, recv2, send3, recv3,
):
    me = lax.axis_index("tm")
    per, total = x_hbm.shape
    half = n // 2
    share = total // half
    frames = n * per
    pack = max(LANES // frames, 1)
    base = jnp.where(me >= half, half, 0)
    place = me - base

    def peer(step):
        there = me + step
        return jnp.where(there >= n, there - n, there)

    def place_of(device):
        return jnp.where(device >= half, device - half, device)

    def mate(step):
        there = place + step
        return jnp.where(there >= half, there - half, there)

    def all_of(buffer, sem):
        blocks = buffer.at[pl.ds(0, buffer.shape[0] - 1)]
        pltpu.make_async_copy(blocks, blocks, sem).wait()

    def share_of(block):
        return pl.ds(pl.multiple_of(block * share, LANES), share)

    def pixel_copy(device, slot):
        return pltpu.make_async_remote_copy(
            src_ref=x_hbm.at[:, share_of(place_of(device))],
            dst_ref=pixels.at[slot],
            send_sem=send1,
            recv_sem=recv1,
            device_id={"tm": device},
            device_id_type=pl.DeviceIdType.MESH,
        )

    def stat_copy(device, slot):
        return pltpu.make_async_remote_copy(
            src_ref=stat_out,
            dst_ref=stat_in.at[slot],
            send_sem=send3,
            recv_sem=recv3,
            device_id={"tm": device},
            device_id_type=pl.DeviceIdType.MESH,
        )

    def part_copy(there):
        return pltpu.make_async_remote_copy(
            src_ref=part_out.at[there],
            dst_ref=part_in.at[place],
            send_sem=send2,
            recv_sem=recv2,
            device_id={"tm": base + there},
            device_id_type=pl.DeviceIdType.MESH,
        )

    loads = [
        pltpu.make_async_copy(source, target, load.at[i])
        for i, (source, target) in enumerate(
            [(label_hbm, label_ref), (mask_hbm, mask_ref), (x_hbm, x_ref), (pair_hbm, pair_ref)]
        )
    ]
    for copy in loads:
        copy.start()
    barrier = pltpu.get_barrier_semaphore()

    for step in range(1, n):
        pl.semaphore_signal(
            barrier, inc=1, device_id={"tm": peer(step)}, device_id_type=pl.DeviceIdType.MESH
        )
    pl.semaphore_wait(barrier, n - 1)
    for step in range(1, n):
        pixel_copy(peer(step), me).start()
    for copy in loads:
        copy.wait()

    pixels[me] = x_ref[:, share_of(place)]
    ones8[...] = jnp.ones_like(ones8)

    def local_sums(block, running):
        where = share_of(block)
        member = member_of(label_ref[:, where], mask_ref[:, where])
        ones8[:per] = x_ref[:, where].astype(jnp.float32)
        return running + lax.dot_general(
            ones8[...].astype(jnp.bfloat16), member, NT, preferred_element_type=jnp.float32
        )

    stats = lax.fori_loop(0, half, local_sums, jnp.zeros((8, CYCLES), jnp.float32))
    stat_out[...] = jnp.zeros_like(stat_out)
    stat_out[:, :CYCLES] = stats
    stat_in[me] = stat_out[...]
    member_own[...] = member_of(label_ref[:, share_of(place)], mask_ref[:, share_of(place)])


    for step in range(1, n):
        stat_copy(peer(step), me).start()

    all_of(pixels, recv1)
    for device in range(n):
        frames32[device * per : (device + 1) * per] = pixels[device].astype(jnp.float32)
    right = frames32[...].astype(jnp.bfloat16)

    def partial(device):
        rows = pixels[device].astype(jnp.float32)
        grams = []
        for f in range(per):
            weighted = member_own[...] * rows[f : f + 1].astype(jnp.bfloat16)
            grams.append(lax.dot_general(weighted, right, NT, preferred_element_type=jnp.float32))
        tiles = [g[8 * c : 8 * c + 8] for g in grams for c in range(GROUPS8)]
        while len(tiles) % pack:
            tiles.append(jnp.zeros((8, frames), jnp.float32))
        return [jnp.concatenate(tiles[i : i + pack], axis=1) for i in range(0, len(tiles), pack)]

    def send_parts(places):
        for there in places:
            for i, tile in enumerate(partial(base + there)):
                part_out[there, 8 * i : 8 * i + 8] = tile
        for there in places:
            part_copy(there).start()

    def send_pair(pair, _):
        send_parts([mate(2 * pair + 1), mate(2 * pair + 2)])
        return 0

    pairs = (half - 1) // 2
    lax.fori_loop(0, pairs, send_pair, 0, unroll=pairs if half <= 8 else 1)
    if (half - 1) % 2:
        send_parts([mate(half - 1)])
    for i, tile in enumerate(partial(me)):
        part_in[place, 8 * i : 8 * i + 8] = tile

    all_of(stat_in, recv3)
    for device in range(n):
        stat_all[device * per : (device + 1) * per] = stat_in[device, :per]
    sums = jnp.transpose(stat_all[...])[:CYCLES]
    own = jnp.transpose(stat_out[...])[:CYCLES]
    blocks = lax.broadcasted_iota(jnp.int32, (n, frames), 0)
    owners = lax.broadcasted_iota(jnp.int32, (n, frames), 1) // per
    spread = jnp.where(blocks == owners, 1.0, 0.0)
    table = pair_ref[...].astype(jnp.float32)
    mine = jnp.where(lax.broadcasted_iota(jnp.int32, (n, n), 0) == me, table, 0.0)
    keep_row = jnp.sum(mine, axis=0, keepdims=True)
    keep = lax.dot_general(
        jnp.broadcast_to(keep_row, (8, n)).astype(jnp.bfloat16),
        spread.astype(jnp.bfloat16),
        (((1,), (0,)), ((), ())),
        preferred_element_type=jnp.float32,
    )[:1]
    counts = own[:, per : per + 1]
    factors = [counts * keep / (own[:, f : f + 1] * sums) for f in range(per)]

    all_of(part_in, recv2)
    for i in range(part_in.shape[1] // 8):
        tile = part_in[0, 8 * i : 8 * i + 8]
        for device in range(1, half):
            tile = tile + part_in[device, 8 * i : 8 * i + 8]
        for b in range(pack):
            f, c = divmod(i * pack + b, GROUPS8)
            if f < per:
                gram = tile[:, b * frames : (b + 1) * frames]
                out_ref[f, 8 * c : 8 * c + 8] = gram * factors[f][8 * c : 8 * c + 8]

    all_of(pixels, send1)
    all_of(stat_in, send3)
    all_of(part_in, send2)


def on_device(n, intensity, cycle_label, pixel_mask, pair_table):
    per, total = intensity.shape
    share = total // (n // 2)
    frames = n * per
    pack = max(LANES // frames, 1)
    rows = -(-per * GROUPS8 // pack) * 8
    width = pack * frames
    vmem = pl.BlockSpec(memory_space=pltpu.VMEM)
    sem = pltpu.SemaphoreType.DMA
    return pl.pallas_call(
        functools.partial(kernel, n),
        out_shape=jax.ShapeDtypeStruct((per, CYCLES, frames), jnp.float32),
        in_specs=[pl.BlockSpec(memory_space=pl.ANY)] * 4,
        out_specs=vmem,
        scratch_shapes=[
            pltpu.VMEM((per, total), jnp.bfloat16),
            pltpu.VMEM((1, total), jnp.int32),
            pltpu.VMEM((1, total), jnp.int32),
            pltpu.VMEM(pair_table.shape, jnp.int32),
            pltpu.VMEM((n, per, share), jnp.bfloat16),
            pltpu.VMEM((frames, share), jnp.float32),
            pltpu.VMEM((n // 2, rows, width), jnp.float32),
            pltpu.VMEM((n // 2, rows, width), jnp.float32),
            pltpu.VMEM((8, LANES), jnp.float32),
            pltpu.VMEM((n, 8, LANES), jnp.float32),
            pltpu.VMEM((frames, LANES), jnp.float32),
            pltpu.VMEM((8, share), jnp.float32),
            pltpu.VMEM((CYCLES, share), jnp.bfloat16),
            pltpu.SemaphoreType.DMA((4,)),
            sem, sem, sem, sem, sem, sem,
        ],
        compiler_params=pltpu.CompilerParams(
            collective_id=0, has_side_effects=True, vmem_limit_bytes=56 * 1024 * 1024
        ),
    )(intensity, cycle_label.reshape(1, total), pixel_mask.reshape(1, total), pair_table)


def solution(mesh):
    in_specs = (P(("groups", "tm"), None), P("groups"), P("groups"), P())
    out_specs = P(("groups", "tm"), None, None)
    return jax.shard_map(
        functools.partial(on_device, mesh.shape["tm"]),
        mesh=mesh, in_specs=in_specs, out_specs=out_specs, check_vma=False,
    )
```

```python
import functools

import jax
import jax.numpy as jnp
from jax import lax
from jax.experimental import pallas as pl
from jax.experimental.pallas import tpu as pltpu
from jax.sharding import PartitionSpec as P

CYCLES = 72
GROUPS8 = CYCLES // 8
LANES = 128
NT = (((1,), (1,)), ((), ()))


def member_of(label, mask):
    key = jnp.where(mask == 1, label, -1)
    ids = lax.broadcasted_iota(jnp.int32, (CYCLES, label.shape[1]), 0)
    return jnp.where(key == ids, 1.0, 0.0).astype(jnp.bfloat16)


def kernel(
    n, x_hbm, label_hbm, mask_hbm, pair_hbm, out_ref,
    x_ref, label_ref, mask_ref, pair_ref, pixels, frames32, part_out, part_in, stat_out, stat_in, stat_all, ones8, member_own,
    load, send1, recv1, send2, recv2, send3, recv3,
):
    me = lax.axis_index("tm")
    per, total = x_hbm.shape
    half = n // 2
    share = total // half
    frames = n * per
    pack = max(LANES // frames, 1)
    base = jnp.where(me >= half, half, 0)
    place = me - base

    def peer(step):
        there = me + step
        return jnp.where(there >= n, there - n, there)

    def place_of(device):
        return jnp.where(device >= half, device - half, device)

    def mate(step):
        there = place + step
        return jnp.where(there >= half, there - half, there)

    def all_of(buffer, sem):
        blocks = buffer.at[pl.ds(0, buffer.shape[0] - 1)]
        pltpu.make_async_copy(blocks, blocks, sem).wait()

    def share_of(block):
        return pl.ds(pl.multiple_of(block * share, LANES), share)

    def pixel_copy(device, slot):
        return pltpu.make_async_remote_copy(
            src_ref=x_ref.at[:, share_of(place_of(device))],
            dst_ref=pixels.at[slot],
            send_sem=send1,
            recv_sem=recv1,
            device_id={"tm": device},
            device_id_type=pl.DeviceIdType.MESH,
        )

    def stat_copy(device, slot):
        return pltpu.make_async_remote_copy(
            src_ref=stat_out,
            dst_ref=stat_in.at[slot],
            send_sem=send3,
            recv_sem=recv3,
            device_id={"tm": device},
            device_id_type=pl.DeviceIdType.MESH,
        )

    def part_copy(there):
        return pltpu.make_async_remote_copy(
            src_ref=part_out.at[there],
            dst_ref=part_in.at[place],
            send_sem=send2,
            recv_sem=recv2,
            device_id={"tm": base + there},
            device_id_type=pl.DeviceIdType.MESH,
        )

    loads = [
        pltpu.make_async_copy(source, target, load.at[i])
        for i, (source, target) in enumerate(
            [(label_hbm, label_ref), (mask_hbm, mask_ref), (x_hbm, x_ref), (pair_hbm, pair_ref)]
        )
    ]
    for copy in loads:
        copy.start()
    barrier = pltpu.get_barrier_semaphore()

    for step in range(1, n):
        pl.semaphore_signal(
            barrier, inc=1, device_id={"tm": peer(step)}, device_id_type=pl.DeviceIdType.MESH
        )
    for copy in loads:
        copy.wait()
    pl.semaphore_wait(barrier, n - 1)
    for step in range(1, n):
        pixel_copy(peer(step), me).start()

    pixels[me] = x_ref[:, share_of(place)]
    ones8[...] = jnp.ones_like(ones8)

    def local_sums(block, running):
        where = share_of(block)
        member = member_of(label_ref[:, where], mask_ref[:, where])
        ones8[:per] = x_ref[:, where].astype(jnp.float32)
        return running + lax.dot_general(
            ones8[...].astype(jnp.bfloat16), member, NT, preferred_element_type=jnp.float32
        )

    stats = lax.fori_loop(0, half, local_sums, jnp.zeros((8, CYCLES), jnp.float32))
    stat_out[...] = jnp.zeros_like(stat_out)
    stat_out[:, :CYCLES] = stats
    stat_in[me] = stat_out[...]
    member_own[...] = member_of(label_ref[:, share_of(place)], mask_ref[:, share_of(place)])


    for step in range(1, n):
        stat_copy(peer(step), me).start()

    all_of(pixels, recv1)
    for device in range(n):
        frames32[device * per : (device + 1) * per] = pixels[device].astype(jnp.float32)
    right = frames32[...].astype(jnp.bfloat16)

    def partial(device):
        rows = pixels[device].astype(jnp.float32)
        grams = []
        for f in range(per):
            weighted = member_own[...] * rows[f : f + 1].astype(jnp.bfloat16)
            grams.append(lax.dot_general(weighted, right, NT, preferred_element_type=jnp.float32))
        tiles = [g[8 * c : 8 * c + 8] for g in grams for c in range(GROUPS8)]
        while len(tiles) % pack:
            tiles.append(jnp.zeros((8, frames), jnp.float32))
        return [jnp.concatenate(tiles[i : i + pack], axis=1) for i in range(0, len(tiles), pack)]

    def send_parts(places):
        for there in places:
            for i, tile in enumerate(partial(base + there)):
                part_out[there, 8 * i : 8 * i + 8] = tile
        for there in places:
            part_copy(there).start()

    def send_pair(pair, _):
        send_parts([mate(2 * pair + 1), mate(2 * pair + 2)])
        return 0

    pairs = (half - 1) // 2
    lax.fori_loop(0, pairs, send_pair, 0, unroll=pairs if half <= 8 else 1)
    if (half - 1) % 2:
        send_parts([mate(half - 1)])
    for i, tile in enumerate(partial(me)):
        part_in[place, 8 * i : 8 * i + 8] = tile

    all_of(stat_in, recv3)
    for device in range(n):
        stat_all[device * per : (device + 1) * per] = stat_in[device, :per]
    sums = jnp.transpose(stat_all[...])[:CYCLES]
    own = jnp.transpose(stat_out[...])[:CYCLES]
    blocks = lax.broadcasted_iota(jnp.int32, (n, frames), 0)
    owners = lax.broadcasted_iota(jnp.int32, (n, frames), 1) // per
    spread = jnp.where(blocks == owners, 1.0, 0.0)
    table = pair_ref[...].astype(jnp.float32)
    mine = jnp.where(lax.broadcasted_iota(jnp.int32, (n, n), 0) == me, table, 0.0)
    keep_row = jnp.sum(mine, axis=0, keepdims=True)
    keep = lax.dot_general(
        jnp.broadcast_to(keep_row, (8, n)).astype(jnp.bfloat16),
        spread.astype(jnp.bfloat16),
        (((1,), (0,)), ((), ())),
        preferred_element_type=jnp.float32,
    )[:1]
    counts = own[:, per : per + 1]
    factors = [counts * keep / (own[:, f : f + 1] * sums) for f in range(per)]

    all_of(part_in, recv2)
    for i in range(part_in.shape[1] // 8):
        tile = part_in[0, 8 * i : 8 * i + 8]
        for device in range(1, half):
            tile = tile + part_in[device, 8 * i : 8 * i + 8]
        for b in range(pack):
            f, c = divmod(i * pack + b, GROUPS8)
            if f < per:
                gram = tile[:, b * frames : (b + 1) * frames]
                out_ref[f, 8 * c : 8 * c + 8] = gram * factors[f][8 * c : 8 * c + 8]

    all_of(pixels, send1)
    all_of(stat_in, send3)
    all_of(part_in, send2)


def on_device(n, intensity, cycle_label, pixel_mask, pair_table):
    per, total = intensity.shape
    share = total // (n // 2)
    frames = n * per
    pack = max(LANES // frames, 1)
    rows = -(-per * GROUPS8 // pack) * 8
    width = pack * frames
    vmem = pl.BlockSpec(memory_space=pltpu.VMEM)
    sem = pltpu.SemaphoreType.DMA
    return pl.pallas_call(
        functools.partial(kernel, n),
        out_shape=jax.ShapeDtypeStruct((per, CYCLES, frames), jnp.float32),
        in_specs=[pl.BlockSpec(memory_space=pl.ANY)] * 4,
        out_specs=vmem,
        scratch_shapes=[
            pltpu.VMEM((per, total), jnp.bfloat16),
            pltpu.VMEM((1, total), jnp.int32),
            pltpu.VMEM((1, total), jnp.int32),
            pltpu.VMEM(pair_table.shape, jnp.int32),
            pltpu.VMEM((n, per, share), jnp.bfloat16),
            pltpu.VMEM((frames, share), jnp.float32),
            pltpu.VMEM((n // 2, rows, width), jnp.float32),
            pltpu.VMEM((n // 2, rows, width), jnp.float32),
            pltpu.VMEM((8, LANES), jnp.float32),
            pltpu.VMEM((n, 8, LANES), jnp.float32),
            pltpu.VMEM((frames, LANES), jnp.float32),
            pltpu.VMEM((8, share), jnp.float32),
            pltpu.VMEM((CYCLES, share), jnp.bfloat16),
            pltpu.SemaphoreType.DMA((4,)),
            sem, sem, sem, sem, sem, sem,
        ],
        compiler_params=pltpu.CompilerParams(
            collective_id=0, has_side_effects=True, vmem_limit_bytes=56 * 1024 * 1024
        ),
    )(intensity, cycle_label.reshape(1, total), pixel_mask.reshape(1, total), pair_table)


def solution(mesh):
    in_specs = (P(("groups", "tm"), None), P("groups"), P("groups"), P())
    out_specs = P(("groups", "tm"), None, None)
    return jax.shard_map(
        functools.partial(on_device, mesh.shape["tm"]),
        mesh=mesh, in_specs=in_specs, out_specs=out_specs, check_vma=False,
    )
```
